32 devices in a mesh: outer: 4 (over x, core), inner: 8 (over z, y).
Axes of the slice: x: 2, y: 2, z: 4, core: 2. Of those that a mesh axis runs over, the one named last changes fastest.
Arguments:
- inputs: bfloat16 [128, 16, 16, 512], P(('outer', 'inner')), may hold values from -12 to 12
- cotangent: bfloat16 [128, 16, 16, 2048], P(('outer', 'inner')), may hold values from -12 to 12
- conv_weight: bfloat16 [4608, 512], replicated, may hold values from -1 to 1
- expand_weight: bfloat16 [512, 2048], replicated, may hold values from -2 to 2
- conv_momentum: float32 [32, 73728], P(('outer', 'inner')), may hold values from -6 to 6
- expand_momentum: float32 [32, 32768], P(('outer', 'inner')), may hold values from -6 to 6
Outputs:
- input_grad: bfloat16 [128, 16, 16, 512], P(('outer', 'inner'))
- conv_new: float32 [32, 73728], P(('outer', 'inner'))
- expand_new: float32 [32, 32768], P(('outer', 'inner'))
The draws below stay inside these ranges and needn't reach their ends.
All inputs are finite; a program needn't handle non-finite values.
Results may differ from the reference program's by a relative error of at most 0.01.
Values may be sent and summed in bfloat16 or wider, within the bound.
No kernel may reach another device: no remote copies, remote signals or barrier semaphores. Data moves between devices by JAX's collectives and lax.ppermute only.
A program may use at most 128 MiB of HBM per device.

```python
import jax
import jax.numpy as jnp
from jax import lax

C = 512
E = 2048
H = 16
W = 16
IMG_DEV = 4
BATCH = 128
S2 = 73728
S3 = 32768
N_OUTER = 4
N_INNER = 8
DEVICES = 32


def mixed_field(key, shape, limit):
    k_common, k_group, k_weight, k_noise, k_scale = jax.random.split(key, 5)
    scales = jnp.exp(jax.random.uniform(k_scale, (shape[-1],), jnp.float32, jnp.log(0.3), jnp.log(3.0)))
    common = jax.random.normal(k_common, shape[1:], jnp.float32)
    group_fields = jax.random.normal(k_group, (N_OUTER,) + tuple(shape[1:]), jnp.float32)
    group_weight = jnp.exp(jax.random.uniform(k_weight, (N_OUTER,), jnp.float32, jnp.log(0.4), jnp.log(1.6)))
    owner = jnp.arange(shape[0]) // IMG_DEV // N_INNER
    own_field = group_fields[owner] * group_weight[owner][:, None, None, None]
    mixture = 0.45 * common + 0.75 * own_field + 0.5 * jax.random.normal(k_noise, shape, jnp.float32)
    return jnp.clip(mixture * scales, -limit, limit)


def channel_levels(key):
    block = C // N_OUTER
    place = (jnp.arange(C) % block).astype(jnp.float32) / block
    jitter = jnp.exp(jax.random.uniform(key, (C,), jnp.float32, jnp.log(0.7), jnp.log(1.4)))
    ratio = 2.2
    return (place, jitter * jnp.exp(jnp.log(ratio) * place))


def kernel_noise(key, shape):
    return jax.random.normal(key, shape, jnp.float32)


def draw_inputs(key, part):
    return mixed_field(jax.random.fold_in(key, 11), (BATCH, H, W, C), 12.0).astype(jnp.bfloat16)


def draw_cotangent(key, part):
    return mixed_field(jax.random.fold_in(key, 23), (BATCH, H, W, E), 12.0).astype(jnp.bfloat16)


def draw_conv_weight(key, part):
    k_noise, k_level = jax.random.split(jax.random.fold_in(key, 37))
    place, level = channel_levels(k_level)
    noise = kernel_noise(k_noise, (9 * C, C))
    kernel = noise * level[None, :] / jnp.sqrt(9.0 * C) + 3.0 * place[None, :] / (9.0 * C)
    return jnp.clip(kernel, -1.0, 1.0).astype(jnp.bfloat16)


def draw_expand_weight(key, part):
    k_noise, k_level = jax.random.split(jax.random.fold_in(key, 41))
    place, level = channel_levels(k_level)
    noise = kernel_noise(k_noise, (C, E))
    kernel = noise * level[:, None] / jnp.sqrt(1.0 * C)
    return jnp.clip(kernel, -2.0, 2.0).astype(jnp.bfloat16)


def levels(stream_key, shape, shards, smallest, top_value):
    loudness = 1.0
    for position, parts in shards:
        draws = jax.random.uniform(jax.random.fold_in(jax.random.fold_in(stream_key, 6), position), (parts,), jnp.float32, smallest / len(shards), top_value / len(shards))
        loudness = loudness * jnp.repeat(jnp.exp(draws), shape[position] // parts).reshape((-1,) + (1,) * (len(shape) - 1 - position))
    return loudness


def centred(rng, dims, deviation, bound, cuts=(), kind=jnp.bfloat16):
    entries = jax.random.normal(rng, dims, jnp.float32) * deviation
    if len(cuts) > 0:
        entries = levels(rng, dims, cuts, -0.22, 0.18) * entries
    return jnp.clip(entries, min=-bound, max=bound).astype(kind)


def setup_inputs(seed: int = 0) -> dict:
    streams_of = jax.random.split(jax.random.key(seed), 7)
    return {
        "inputs": draw_inputs(jax.random.fold_in(streams_of[6], 71), 0),
        "cotangent": draw_cotangent(jax.random.fold_in(streams_of[6], 71), 0),
        "conv_weight": draw_conv_weight(jax.random.fold_in(streams_of[6], 71), 0),
        "expand_weight": draw_expand_weight(jax.random.fold_in(streams_of[6], 71), 0),
        "conv_momentum": centred(streams_of[4], (DEVICES, S2), 1.0, 6.0, ((0, 32),), jnp.float32),
        "expand_momentum": centred(streams_of[5], (DEVICES, S3), 1.0, 6.0, ((0, 32),), jnp.float32),
    }


EPS = 1e-6
MOMENTUM = 0.9


def patches(image):
    images, height, across, channels = image.shape
    padded = jnp.pad(image, ((0, 0), (1, 1), (1, 1), (0, 0)))
    pieces = [padded[:, shift_y:shift_y + height, shift_x:shift_x + across, :] for shift_y in range(3) for shift_x in range(3)]
    return jnp.concatenate(pieces, axis=-1).reshape(images * height * across, 9 * channels)


def local_step(inputs, cotangent, conv_weight, expand_weight):
    images, height, across, channels = inputs.shape
    row_count = images * height * across
    relu_in = jnp.maximum(inputs, jnp.zeros((), inputs.dtype))
    columns = patches(relu_in)
    hidden_pre = jnp.dot(columns, conv_weight, preferred_element_type=jnp.float32).astype(jnp.bfloat16)
    hidden_act = jnp.maximum(hidden_pre, jnp.zeros((), hidden_pre.dtype))
    grad_rows = cotangent.reshape(row_count, cotangent.shape[-1])
    expand_grad = (lax.dot_general(hidden_act, grad_rows, (((0,), (0,)), ((), ())), preferred_element_type=jnp.float32) / row_count).astype(jnp.bfloat16)
    hidden_back = lax.dot_general(grad_rows, expand_weight, (((1,), (1,)), ((), ())), preferred_element_type=jnp.float32)
    hidden_grad = jnp.where(hidden_pre > 0, hidden_back, 0.0).astype(jnp.bfloat16)
    conv_grad = (lax.dot_general(columns, hidden_grad, (((0,), (0,)), ((), ())), preferred_element_type=jnp.float32) / row_count).astype(jnp.bfloat16)
    flipped = conv_weight.reshape(3, 3, channels, channels)[::-1, ::-1].transpose(0, 1, 3, 2).reshape(9 * channels, channels)
    back_cols = patches(hidden_grad.reshape(images, height, across, channels))
    input_back = jnp.dot(back_cols, flipped, preferred_element_type=jnp.float32)
    input_grad = jnp.where(inputs.reshape(row_count, channels) > 0, input_back, 0.0).astype(jnp.bfloat16)
    return input_grad.reshape(inputs.shape), conv_grad, expand_grad


def adasum_levels(vectors):
    outer_count = vectors.shape[0]
    group_span = 1
    while group_span < outer_count:
        grouped = vectors.reshape(outer_count // (2 * group_span), 2, group_span, vectors.shape[1])
        low_side = grouped[:, 0]
        high_side = grouped[:, 1]
        norm_low = jnp.sum(low_side * low_side, axis=-1, keepdims=True)
        norm_high = jnp.sum(high_side * high_side, axis=-1, keepdims=True)
        cross_dot = jnp.sum(low_side * high_side, axis=-1, keepdims=True)
        merged = (1.0 - cross_dot / (2.0 * (norm_low + EPS))) * low_side + (1.0 - cross_dot / (2.0 * (norm_high + EPS))) * high_side
        vectors = jnp.stack([merged, merged], axis=1).reshape(outer_count, vectors.shape[1])
        group_span = group_span * 2
    return vectors[0]


def reference(inputs, cotangent, conv_weight, expand_weight, conv_momentum, expand_momentum):
    device_inputs = inputs.reshape(N_OUTER, N_INNER, IMG_DEV, H, W, C)
    device_cot = cotangent.reshape(N_OUTER, N_INNER, IMG_DEV, H, W, E)

    def outer_fn(pair):
        inputs_outer, cot_outer = pair
        conv_sum = jnp.zeros((9 * C * C,), jnp.float32)
        expand_sum = jnp.zeros((C * E,), jnp.float32)
        grads_list = []
        for inner_pos in range(N_INNER):
            input_grad, conv_grad, expand_grad = local_step(inputs_outer[inner_pos], cot_outer[inner_pos], conv_weight, expand_weight)
            conv_sum = conv_sum + conv_grad.T.reshape(-1).astype(jnp.float32)
            expand_sum = expand_sum + expand_grad.reshape(-1).astype(jnp.float32)
            grads_list.append(input_grad)
        return jnp.stack(grads_list), conv_sum, expand_sum

    all_grads, conv_stack, expand_stack = lax.map(outer_fn, (device_inputs, device_cot))
    conv_final = adasum_levels(conv_stack)
    expand_final = adasum_levels(expand_stack)
    conv_new = MOMENTUM * conv_momentum + conv_final.reshape(DEVICES, S2)
    expand_new = MOMENTUM * expand_momentum + expand_final.reshape(DEVICES, S3)
    return all_grads.reshape(BATCH, H, W, C), conv_new, expand_new
```

```python
import functools

import jax
import jax.numpy as jnp
from jax import lax
from jax.experimental import pallas as pl
from jax.experimental.pallas import tpu as pltpu
from jax.sharding import PartitionSpec as P

EPS = 1e-06
MOMENTUM = 0.9
LANES = 128
VMEM = 48 * 1024 * 1024


def params(**more):
    return pltpu.CompilerParams(vmem_limit_bytes=VMEM, **more)


def cost(macs, moved):
    return pl.CostEstimate(flops=2 * macs, bytes_accessed=moved, transcendentals=0)


def exchange(block, axis, bit):
    count = lax.axis_size(axis)
    return lax.ppermute(block, axis, [(i, i ^ (1 << bit)) for i in range(count)])


def my_bit(axis, bit):
    return (lax.axis_index(axis) >> bit) & 1


def fill_row_taps(source_ref, taps_ref, images, height, across, relu):
    channels = source_ref.shape[1]
    area = height * across
    for image in range(images):
        base = image * area
        block = source_ref[base : base + area, :]
        if relu:
            block = jnp.maximum(block, jnp.zeros((), block.dtype))
        blank = jnp.zeros((across, channels), block.dtype)
        taps_ref[base : base + across, 0:channels] = blank
        taps_ref[base + across : base + area, 0:channels] = block[: area - across]
        taps_ref[base : base + area, channels : 2 * channels] = block
        taps_ref[base : base + area - across, 2 * channels : 3 * channels] = block[across:]
        taps_ref[base + area - across : base + area, 2 * channels : 3 * channels] = blank


def shifted_sum(product, across):
    rows, width = product(1).shape
    place = lax.rem(lax.broadcasted_iota(jnp.int32, (rows, width), 0), across)
    total = product(1)
    total += jnp.where(place > 0, pltpu.roll(product(0), 1, 0), 0.0)
    total += jnp.where(place < across - 1, pltpu.roll(product(2), rows - 1, 0), 0.0)
    return total


def forward_kernel(images, height, across, x_ref, w_ref, out_ref, taps_ref):
    channels = x_ref.shape[1]

    @pl.when(pl.program_id(0) == 0)
    def _():
        fill_row_taps(x_ref, taps_ref, images, height, across, True)

    @functools.cache
    def product(tap_x):
        weight = jnp.concatenate(
            [w_ref[(3 * tap_y + tap_x) * channels : (3 * tap_y + tap_x + 1) * channels, :] for tap_y in range(3)],
            axis=0,
        )
        return jnp.dot(taps_ref[...], weight, preferred_element_type=jnp.float32)

    out_ref[...] = shifted_sum(product, across).astype(out_ref.dtype)


def forward(x, weight, shape):
    images, height, across, channels = shape
    rows = images * height * across
    wide = weight.shape[1]
    block = wide // 2
    return pl.pallas_call(
        functools.partial(forward_kernel, images, height, across),
        out_shape=jax.ShapeDtypeStruct((rows, wide), jnp.bfloat16),
        grid=(2,),
        in_specs=[
            pl.BlockSpec((rows, channels), lambda n: (0, 0)),
            pl.BlockSpec((9 * channels, block), lambda n: (0, n)),
        ],
        out_specs=pl.BlockSpec((rows, block), lambda n: (0, n)),
        scratch_shapes=[pltpu.VMEM((rows, 3 * channels), jnp.bfloat16)],
        compiler_params=params(),
        cost_estimate=cost(rows * 9 * channels * wide, 2 * (weight.size + 2 * rows * channels)),
        name="conv_forward",
    )(x, weight)


def backward_kernel(images, height, across, d_ref, w_ref, x_ref, out_ref, taps_ref):
    @pl.when(pl.program_id(0) == 0)
    def _():
        fill_row_taps(d_ref, taps_ref, images, height, across, False)

    @functools.cache
    def product(tap_x):
        weight = jnp.concatenate([w_ref[3 * (2 - tap_y) + 2 - tap_x] for tap_y in range(3)], axis=1)
        return lax.dot_general(
            taps_ref[...], weight, (((1,), (1,)), ((), ())), preferred_element_type=jnp.float32
        )

    total = shifted_sum(product, across)
    keep = x_ref[...].astype(jnp.float32) > 0
    out_ref[...] = jnp.where(keep, total, 0.0).astype(out_ref.dtype)


def backward(hidden_grad, weight, x, shape):
    images, height, across, channels = shape
    rows = images * height * across
    wide = weight.shape[1]
    block = channels // 2
    return pl.pallas_call(
        functools.partial(backward_kernel, images, height, across),
        out_shape=jax.ShapeDtypeStruct((rows, channels), jnp.bfloat16),
        grid=(2,),
        in_specs=[
            pl.BlockSpec((rows, wide), lambda n: (0, 0)),
            pl.BlockSpec((9, block, wide), lambda n: (0, n, 0)),
            pl.BlockSpec((rows, block), lambda n: (0, n)),
        ],
        out_specs=pl.BlockSpec((rows, block), lambda n: (0, n)),
        scratch_shapes=[pltpu.VMEM((rows, 3 * wide), jnp.bfloat16)],
        compiler_params=params(),
        cost_estimate=cost(rows * 9 * channels * wide, 2 * (weight.size + 3 * rows * channels)),
        name="conv_backward",
    )(hidden_grad, weight.reshape(9, channels, wide), x)


def kernel_grad_kernel(images, height, across, tap_y, xa_ref, xb_ref, da_ref, db_ref, out_ref, x_ref, d_ref):
    rows, channels = xa_ref.shape
    area = height * across
    for source, ref in enumerate((xa_ref, xb_ref)):
        for image in range(images):
            base = image * area
            block = ref[base : base + area, :]
            block = jnp.maximum(block, jnp.zeros((), block.dtype))
            blank = jnp.zeros((across, channels), block.dtype)
            base += source * rows
            if tap_y == 0:
                x_ref[base : base + across, :] = blank
                x_ref[base + across : base + area, :] = block[: area - across]
            elif tap_y == 1:
                x_ref[base : base + area, :] = block
            else:
                x_ref[base : base + area - across, :] = block[across:]
                x_ref[base + area - across : base + area, :] = blank
    place = lax.rem(lax.broadcasted_iota(jnp.int32, da_ref.shape, 1), across)
    for tap_x in range(3):
        for source, ref in enumerate((da_ref, db_ref)):
            block = ref[...]
            if tap_x != 1:
                wide = pltpu.roll(block.astype(jnp.float32), (tap_x - 1) % rows, 1)
                valid = place < across - 1 if tap_x == 0 else place > 0
                block = jnp.where(valid, wide, 0.0).astype(block.dtype)
            d_ref[:, source * rows : (source + 1) * rows] = block
        total = jnp.dot(d_ref[...], x_ref[...], preferred_element_type=jnp.float32)
        out_ref[:, tap_x * channels : (tap_x + 1) * channels] = (total / rows).astype(out_ref.dtype)


def kernel_grad(tap_y, x_own, x_other, d_own, d_other, shape):
    images, height, across, channels = shape
    rows = images * height * across
    half = d_own.shape[0]
    return pl.pallas_call(
        functools.partial(kernel_grad_kernel, images, height, across, tap_y),
        out_shape=jax.ShapeDtypeStruct((half, 3 * channels), jnp.bfloat16),
        scratch_shapes=[
            pltpu.VMEM((2 * rows, channels), jnp.bfloat16),
            pltpu.VMEM((half, 2 * rows), jnp.bfloat16),
        ],
        compiler_params=params(),
        cost_estimate=cost(2 * rows * 3 * channels * half, 4 * rows * (channels + half) + 6 * half * channels),
        name=f"conv_grad_rows{tap_y}",
    )(x_own, x_other, d_own, d_other)


def pairs_of(count):
    return [(a, b) for a in range(count) for b in range(a, count)]


def stat_rows(count):
    return -(-len(pairs_of(count)) // 8) * 8


def gram_kernel(offset, *refs):
    v_ref, out_ref = refs[0], refs[-1]
    count, rows, width = v_ref.shape
    if len(refs) == 3:
        out_ref[...] = refs[1][...]
    else:
        out_ref[...] = jnp.zeros(out_ref.shape, jnp.float32)
    vectors = [v_ref[o].astype(jnp.float32) for o in range(count)]
    for index, (a, b) in enumerate(pairs_of(count)):
        product = vectors[a] * vectors[b]
        folded = sum(product[:, g : g + LANES] for g in range(0, width, LANES))
        row = offset + index
        out_ref[row : row + 1, :] += jnp.sum(folded, axis=0, keepdims=True)


def gram(vectors, offset, before):
    count = vectors.shape[0]
    args = (vectors,) if before is None else (vectors, before)
    return pl.pallas_call(
        functools.partial(gram_kernel, offset),
        out_shape=jax.ShapeDtypeStruct((2 * stat_rows(count), LANES), jnp.float32),
        compiler_params=params(),
        name="gram",
    )(*args)


def adasum_coefs(table, count):
    def dot(first, second):
        total = 0.0
        for i, u in first.items():
            for j, v in second.items():
                total = total + u * v * table[min(i, j), max(i, j)]
        return total

    held = [{o: jnp.ones((1, LANES), jnp.float32)} for o in range(count)]
    while len(held) > 1:
        merged = []
        for low, high in zip(held[::2], held[1::2]):
            cross = dot(low, high)
            low_coef = 1.0 - cross / (2.0 * (jnp.maximum(dot(low, low), 0.0) + EPS))
            high_coef = 1.0 - cross / (2.0 * (jnp.maximum(dot(high, high), 0.0) + EPS))
            both = {o: low_coef * u for o, u in low.items()}
            both.update({o: high_coef * u for o, u in high.items()})
            merged.append(both)
        held = merged
    return held[0]


def finish_kernel(pieces, *refs):
    stats_ref = refs[0]
    conv_refs = refs[1 : 1 + pieces]
    expand_ref, conv_m_ref, expand_m_ref, conv_out, expand_out = refs[1 + pieces :]
    count, rows, _ = expand_ref.shape

    def apply(offset, v_refs, m_ref, out_ref):
        table = {}
        for index, pair in enumerate(pairs_of(count)):
            lane = stats_ref[offset + index : offset + index + 1, :]
            table[pair] = jnp.broadcast_to(jnp.sum(lane, axis=1, keepdims=True), (1, LANES))
        coefs = adasum_coefs(table, count)
        stride = sum(ref.shape[2] for ref in v_refs) // LANES
        group = 0
        for ref in v_refs:
            for start in range(0, ref.shape[2], LANES):
                total = sum(
                    coefs[o] * ref[o, :, start : start + LANES].astype(jnp.float32) for o in range(count)
                )
                place = pl.ds(group, rows, stride=stride)
                out_ref[place, :] = MOMENTUM * m_ref[place, :] + total
                group += 1

    apply(0, conv_refs, conv_m_ref, conv_out)
    apply(stat_rows(count), (expand_ref,), expand_m_ref, expand_out)


def finish(stats, conv_pieces, expand, conv_momentum, expand_momentum):
    conv_m = conv_momentum.reshape(-1, LANES)
    expand_m = expand_momentum.reshape(-1, LANES)
    conv_new, expand_new = pl.pallas_call(
        functools.partial(finish_kernel, len(conv_pieces)),
        out_shape=(
            jax.ShapeDtypeStruct(conv_m.shape, jnp.float32),
            jax.ShapeDtypeStruct(expand_m.shape, jnp.float32),
        ),
        compiler_params=params(),
        name="finish",
    )(stats, *conv_pieces, expand, conv_m, expand_m)
    return conv_new.reshape(conv_momentum.shape), expand_new.reshape(expand_momentum.shape)


def halve(block, dim, bit):
    mine = my_bit("inner", bit)
    send = lax.dynamic_index_in_dim(block, 1 - mine, dim, keepdims=False)
    keep = lax.dynamic_index_in_dim(block, mine, dim, keepdims=False)
    got = exchange(send, "inner", bit)
    return (keep.astype(jnp.float32) + got.astype(jnp.float32)).astype(jnp.bfloat16)


def reduce_over_inner(block, order, bits):
    left = sorted(bits, reverse=True)
    for bit in order:
        block = halve(block, 1 + left.index(bit), bit)
        left.remove(bit)
    return block


def all_to_all_outer(block):
    count = lax.axis_size("outer")
    levels = count.bit_length() - 1
    tail = block.shape[1:]
    block = block.reshape((2,) * levels + tail)
    for bit in reversed(range(levels)):
        dim = levels - 1 - bit
        mine = my_bit("outer", bit)
        send = lax.dynamic_index_in_dim(block, 1 - mine, dim, keepdims=False)
        keep = lax.dynamic_index_in_dim(block, mine, dim, keepdims=False)
        got = exchange(send, "outer", bit)
        low = jnp.where(mine == 0, keep, got)
        high = jnp.where(mine == 0, got, keep)
        block = jnp.stack([low, high], axis=dim)
    return block.reshape((count,) + tail)


def body(inputs, cotangent, conv_weight, expand_weight, conv_momentum, expand_momentum):
    shape = inputs.shape
    images, height, across, channels = shape
    rows = images * height * across
    wide = cotangent.shape[-1]
    outer_count = lax.axis_size("outer")
    inner_count = lax.axis_size("inner")
    inner_bits = inner_count.bit_length() - 1
    outer_bits = outer_count.bit_length() - 1
    hidden = conv_weight.shape[1]
    own = hidden // (outer_count * inner_count)

    x_own = inputs.reshape(rows, channels)
    x_other = exchange(x_own, "inner", 0)
    hidden_pre = forward(x_own, conv_weight, shape)
    hidden_act = jnp.maximum(hidden_pre, jnp.zeros((), hidden_pre.dtype))
    grad_rows = cotangent.reshape(rows, wide)
    expand_grad = (
        lax.dot_general(
            hidden_act, grad_rows, (((0,), (0,)), ((), ())), preferred_element_type=jnp.float32
        )
        / rows
    ).astype(jnp.bfloat16)
    hidden_back = lax.dot_general(
        grad_rows, expand_weight, (((1,), (1,)), ((), ())), preferred_element_type=jnp.float32
    )
    hidden_grad = jnp.where(hidden_pre > 0, hidden_back, 0.0).astype(jnp.bfloat16)

    twos = (2,) * inner_bits
    expand_order = list(range(1, inner_bits))
    expand_order.insert(1, 0)
    expand_own = reduce_over_inner(
        expand_grad.reshape((outer_count,) + twos + (own, wide)), expand_order, range(inner_bits)
    )

    grad_t = hidden_grad.T.reshape((outer_count * inner_count // 2, 2, own, rows))
    side = my_bit("inner", 0)
    d_own = lax.dynamic_index_in_dim(grad_t, side, 1, keepdims=False).reshape(hidden // 2, rows)
    d_send = lax.dynamic_index_in_dim(grad_t, 1 - side, 1, keepdims=False).reshape(hidden // 2, rows)
    d_other = exchange(d_send, "inner", 0)

    input_grad = backward(hidden_grad, conv_weight, x_own, shape).reshape(shape)

    conv_owns = []
    for tap_y in range(3):
        piece = kernel_grad(tap_y, x_own, x_other, d_own, d_other, shape)
        piece = piece.reshape((outer_count,) + twos[1:] + (own, 3 * channels))
        conv_owns.append(reduce_over_inner(piece, range(1, inner_bits), range(1, inner_bits)))

    expand_all = all_to_all_outer(expand_own)
    stats = gram(expand_all, stat_rows(outer_count), None)
    conv_alls = []
    for piece in conv_owns:
        conv_alls.append(all_to_all_outer(piece))
        stats = gram(conv_alls[-1], 0, stats)
    for axis, bits in (("inner", inner_bits), ("outer", outer_bits)):
        for bit in range(bits):
            stats = stats + exchange(stats, axis, bit)
    conv_new, expand_new = finish(stats, conv_alls, expand_all, conv_momentum, expand_momentum)
    return (input_grad, conv_new, expand_new)


def solution(mesh):
    split = P(("outer", "inner"))
    return jax.shard_map(
        body,
        mesh=mesh,
        in_specs=(split, split, P(), P(), split, split),
        out_specs=(split, split, split),
        check_vma=False,
    )
```

```python
import functools

import jax
import jax.numpy as jnp
from jax import lax
from jax.experimental import pallas as pl
from jax.experimental.pallas import tpu as pltpu
from jax.sharding import PartitionSpec as P

EPS = 1e-06
MOMENTUM = 0.9
LANES = 128
VMEM = 48 * 1024 * 1024


def params(**more):
    return pltpu.CompilerParams(vmem_limit_bytes=VMEM, **more)


def call(kernel, name, out_shape, args, after=(), scratch=(), in_specs=None):
    count = len(args)

    def run(*refs):
        kernel(*refs[:count], *refs[count + len(after) :])

    if in_specs is None:
        in_specs = [pl.BlockSpec(memory_space=pltpu.VMEM)] * count
    return pl.pallas_call(
        run,
        out_shape=out_shape,
        in_specs=list(in_specs) + [pl.BlockSpec(memory_space=pl.ANY)] * len(after),
        scratch_shapes=list(scratch),
        compiler_params=params(),
        cost_estimate=pl.CostEstimate(flops=1, bytes_accessed=1, transcendentals=0),
        name=name,
    )(*args, *after)


def half(shape):
    return jax.ShapeDtypeStruct(shape, jnp.bfloat16)


def exchange(block, axis, bit):
    count = lax.axis_size(axis)
    return lax.ppermute(block, axis, [(i, i ^ (1 << bit)) for i in range(count)])


def my_bit(axis, bit):
    return (lax.axis_index(axis) >> bit) & 1


def fill_row_taps(source_ref, taps_ref, images, height, across, relu):
    channels = source_ref.shape[1]
    area = height * across
    for image in range(images):
        base = image * area
        block = source_ref[base : base + area, :]
        if relu:
            block = jnp.maximum(block, jnp.zeros((), block.dtype))
        blank = jnp.zeros((across, channels), block.dtype)
        taps_ref[base : base + across, 0:channels] = blank
        taps_ref[base + across : base + area, 0:channels] = block[: area - across]
        taps_ref[base : base + area, channels : 2 * channels] = block
        taps_ref[base : base + area - across, 2 * channels : 3 * channels] = block[across:]
        taps_ref[base + area - across : base + area, 2 * channels : 3 * channels] = blank


def shifted_sum(product, across):
    rows, width = product(1).shape
    place = lax.rem(lax.broadcasted_iota(jnp.int32, (rows, width), 0), across)
    total = product(1)
    total += jnp.where(place > 0, pltpu.roll(product(0), 1, 0), 0.0)
    total += jnp.where(place < across - 1, pltpu.roll(product(2), rows - 1, 0), 0.0)
    return total


def store_split(value, bit, step, send_ref, keep_ref, first, columns):
    mine = my_bit("inner", bit)
    for pair in range(value.shape[0] // (2 * step)):
        zero = value[2 * pair * step : (2 * pair + 1) * step]
        one = value[(2 * pair + 1) * step : (2 * pair + 2) * step]
        place = slice(first + pair * step, first + (pair + 1) * step)
        keep_ref[place, columns] = jnp.where(mine == 0, zero, one).astype(keep_ref.dtype)
        send_ref[place, columns] = jnp.where(mine == 0, one, zero).astype(send_ref.dtype)


def split_rows(block, bit, step):
    mine = my_bit("inner", bit)
    parts = block.reshape(block.shape[0] // (2 * step), 2, step, block.shape[1])
    send = lax.dynamic_index_in_dim(parts, 1 - mine, 1, keepdims=False)
    keep = lax.dynamic_index_in_dim(parts, mine, 1, keepdims=False)
    return [part.reshape(block.shape[0] // 2, block.shape[1]) for part in (send, keep)]


def fused_split(own):
    return own % 16 == 0


def front_kernel(index, bit, own, shape, x_hbm, w_hbm, cot_hbm, *refs):
    images, height, across, channels = shape
    hid_ref, *out_refs = refs[:-5]
    x_ref, w_ref, cot_ref, taps_ref, sems = refs[-5:]
    rows, block = hid_ref.shape
    x_copy = pltpu.make_async_copy(x_hbm, x_ref, sems.at[0])
    cot_copy = pltpu.make_async_copy(cot_hbm, cot_ref, sems.at[1])
    w_copies = {}
    for tap_x in (1, 0, 2):
        for tap_y in range(3):
            tap = 3 * tap_y + tap_x
            w_copies[tap] = pltpu.make_async_copy(
                w_hbm.at[pl.ds(tap * channels, channels), pl.ds(index * block, block)],
                w_ref.at[pl.ds(tap * channels, channels), :],
                sems.at[2 + tap],
            )
    x_copy.start()
    for copy in w_copies.values():
        copy.start()
    cot_copy.start()
    x_copy.wait()
    fill_row_taps(x_ref, taps_ref, images, height, across, True)

    @functools.cache
    def product(tap_x):
        for tap_y in range(3):
            w_copies[3 * tap_y + tap_x].wait()
        weight = jnp.concatenate(
            [w_ref[(3 * tap_y + tap_x) * channels : (3 * tap_y + tap_x + 1) * channels, :] for tap_y in range(3)],
            axis=0,
        )
        return jnp.dot(taps_ref[...], weight, preferred_element_type=jnp.float32)

    hidden = shifted_sum(product, across).astype(hid_ref.dtype)
    hid_ref[...] = hidden
    act = jnp.maximum(hidden, jnp.zeros((), hidden.dtype))
    cot_copy.wait()
    wide = cot_ref.shape[1]
    piece = min(wide, 512)
    for start in range(0, wide, piece):
        columns = slice(start, start + piece)
        grad = lax.dot_general(
            act, cot_ref[:, columns], (((0,), (0,)), ((), ())), preferred_element_type=jnp.float32
        )
        grad = grad / rows
        if len(out_refs) == 2:
            store_split(grad, bit, own << bit, *out_refs, 0, columns)
        else:
            out_refs[0][:, columns] = grad.astype(jnp.bfloat16)


def front(index, x, weight, cot, shape, bit, own):
    rows, channels = x.shape
    wide = cot.shape[1]
    block = weight.shape[1] // 2
    parts = 2 if fused_split(own) else 1
    hidden, *grads = call(
        functools.partial(front_kernel, index, bit, own, shape),
        f"forward_expand{index}",
        [half((rows, block))] + [half((block // parts, wide))] * parts,
        (x, weight, cot),
        in_specs=[pl.BlockSpec(memory_space=pl.ANY)] * 3,
        scratch=[
            pltpu.VMEM((rows, channels), jnp.bfloat16),
            pltpu.VMEM((9 * channels, block), jnp.bfloat16),
            pltpu.VMEM((rows, wide), jnp.bfloat16),
            pltpu.VMEM((rows, 3 * channels), jnp.bfloat16),
            pltpu.SemaphoreType.DMA((11,)),
        ],
    )
    if parts == 1:
        grads = split_rows(grads[0], bit, own << bit)
    return hidden, *grads


def hidden_grad_kernel(own, *refs):
    blocks = refs[:2]
    cot_ref, w_ref, out_ref, *t_refs = refs[2:]
    wide = blocks[0].shape[1]
    for index, hid_ref in enumerate(blocks):
        place = slice(index * wide, (index + 1) * wide)
        back = lax.dot_general(
            cot_ref[...], w_ref[place, :], (((1,), (1,)), ((), ())), preferred_element_type=jnp.float32
        )
        grad = jnp.where(hid_ref[...].astype(jnp.float32) > 0, back, 0.0)
        out_ref[:, place] = grad.astype(out_ref.dtype)
        turned = grad.T
        if len(t_refs) == 2:
            store_split(turned, 0, own, *t_refs, index * wide // 2, slice(None))
        else:
            t_refs[0][place, :] = turned.astype(jnp.bfloat16)


def hidden_gradient(hidden, cot, weight, own, after):
    rows, block = hidden[0].shape
    wide = 2 * block
    parts = 2 if fused_split(own) else 1
    grad, *turned = call(
        functools.partial(hidden_grad_kernel, own),
        "hidden_grad",
        [half((rows, wide))] + [half((wide // parts, rows))] * parts,
        (*hidden, cot, weight),
        after,
    )
    if parts == 1:
        turned = split_rows(turned[0], 0, own)
    return grad, *turned


def backward_kernel(shape, d_ref, w_ref, x_ref, out_ref, taps_ref):
    images, height, across, channels = shape
    fill_row_taps(d_ref, taps_ref, images, height, across, False)
    block = channels // 2
    for start in range(0, channels, block):
        columns = slice(start, start + block)

        @functools.cache
        def product(tap_x):
            weight = jnp.concatenate(
                [w_ref[3 * (2 - tap_y) + 2 - tap_x, columns, :] for tap_y in range(3)], axis=1
            )
            return lax.dot_general(
                taps_ref[...], weight, (((1,), (1,)), ((), ())), preferred_element_type=jnp.float32
            )

        total = shifted_sum(product, across)
        keep = x_ref[:, columns].astype(jnp.float32) > 0
        out_ref[:, columns] = jnp.where(keep, total, 0.0).astype(out_ref.dtype)


def backward(hidden_grad, weight, x, shape):
    rows, channels = x.shape
    wide = weight.shape[1]
    return call(
        functools.partial(backward_kernel, shape),
        "conv_backward",
        half((rows, channels)),
        (hidden_grad, weight.reshape(9, channels, wide), x),
        scratch=[pltpu.VMEM((rows, 3 * wide), jnp.bfloat16)],
    )


def kernel_grad_kernel(tap_y, bit, step, shape, x_count, *refs):
    images, height, across, channels = shape
    area = height * across
    x_refs = refs[:x_count]
    d_refs = refs[x_count : x_count + 2]
    out_refs = refs[x_count + 2 : -2]
    x_ref, d_ref = refs[-2:]
    rows = d_refs[0].shape[1]
    first = 0
    for ref in x_refs:
        for image in range(ref.shape[0] // area):
            block = ref[image * area : (image + 1) * area, :]
            block = jnp.maximum(block, jnp.zeros((), block.dtype))
            blank = jnp.zeros((across, channels), block.dtype)
            if tap_y == 0:
                x_ref[first : first + across, :] = blank
                x_ref[first + across : first + area, :] = block[: area - across]
            elif tap_y == 1:
                x_ref[first : first + area, :] = block
            else:
                x_ref[first : first + area - across, :] = block[across:]
                x_ref[first + area - across : first + area, :] = blank
            first += area
    place = lax.rem(lax.broadcasted_iota(jnp.int32, d_refs[0].shape, 1), across)
    for tap_x in range(3):
        for source, ref in enumerate(d_refs):
            block = ref[...]
            if tap_x != 1:
                wide = pltpu.roll(block.astype(jnp.float32), (tap_x - 1) % rows, 1)
                valid = place < across - 1 if tap_x == 0 else place > 0
                block = jnp.where(valid, wide, 0.0).astype(block.dtype)
            d_ref[:, source * rows : (source + 1) * rows] = block
        total = jnp.dot(d_ref[...], x_ref[...], preferred_element_type=jnp.float32) / rows
        columns = slice(tap_x * channels, (tap_x + 1) * channels)
        if len(out_refs) == 2:
            store_split(total, bit, step, *out_refs, 0, columns)
        else:
            out_refs[0][:, columns] = total.astype(jnp.bfloat16)


def kernel_grad(tap_y, xs, ds, shape, bit, own, after):
    channels = shape[3]
    wide, rows = ds[0].shape
    parts = 2 if fused_split(own) else 1
    grads = call(
        functools.partial(kernel_grad_kernel, tap_y, bit, own << (bit - 1), shape, len(xs)),
        f"conv_grad_rows{tap_y}",
        [half((wide // parts, 3 * channels))] * parts,
        (*xs, *ds),
        after,
        scratch=[
            pltpu.VMEM((2 * rows, channels), jnp.bfloat16),
            pltpu.VMEM((wide, 2 * rows), jnp.bfloat16),
        ],
    )
    if parts == 1:
        grads = split_rows(grads[0], bit, own << (bit - 1))
    return grads


def merge_kernel(axis, bit, *refs):
    count = (len(refs) - 2) // 2
    send_ref, keep_ref = refs[-2:]
    mine = my_bit(axis, bit)
    first = 0
    for index in range(count):
        kept, got = refs[2 * index : 2 * index + 2]
        last = first + kept.shape[0]
        for out_ref, side in ((keep_ref, mine), (send_ref, 1 - mine)):
            total = kept[:, side].astype(jnp.float32) + got[:, side].astype(jnp.float32)
            out_ref[first:last] = total.astype(out_ref.dtype)
        first = last


def merge(parts, leading, axis, bit, after=(), name="merge"):
    flat = []
    for kept, got, lead in zip(*zip(*parts), leading):
        for block in (kept, got):
            flat.append(block.reshape((lead, 2, -1) + block.shape[-2:]))
    lead, _, middle, own, wide = flat[0].shape
    out = half((sum(leading), middle, own, wide))
    return call(functools.partial(merge_kernel, axis, bit), name, [out] * 2, flat, after)


def spread_kernel(bit, kept, got, send_ref, keep_ref):
    mine = my_bit("outer", bit)
    sources = kept.shape[0]
    for index, ref in enumerate((kept, got)):
        place = slice(index * sources, (index + 1) * sources)
        keep_ref[place] = ref[:, mine]
        send_ref[place] = ref[:, 1 - mine]


def spread(kept, got, bit, after=()):
    sources, left, own, wide = kept.shape
    out = half((2 * sources, left // 2, own, wide))
    args = [block.reshape(sources, 2, left // 2, own, wide) for block in (kept, got)]
    return call(functools.partial(spread_kernel, bit), "spread", [out] * 2, args, after)


def gram_kernel(offset, *refs):
    kept, got = refs[:2]
    v_ref, out_ref = refs[-2:]
    sources, rows, width = kept.shape
    count = 2 * sources
    levels = count.bit_length() - 1
    vectors = [None] * count
    for index in range(count):
        flips = sum(((index >> k) & 1) << (levels - 1 - k) for k in range(levels))
        vectors[flips] = (kept if index < sources else got)[index % sources].astype(jnp.float32)
    for bit in range(levels):
        mine = my_bit("outer", bit)
        for low in range(count):
            high = low | 1 << bit
            if high != low:
                a, b = vectors[low], vectors[high]
                vectors[low] = jnp.where(mine == 0, a, b)
                vectors[high] = jnp.where(mine == 0, b, a)
    for index, vector in enumerate(vectors):
        v_ref[index] = vector.astype(v_ref.dtype)
    if len(refs) == 5:
        out_ref[...] = refs[2][...]
    else:
        out_ref[...] = jnp.zeros(out_ref.shape, jnp.float32)
    for index, (a, b) in enumerate(pairs_of(count)):
        product = vectors[a] * vectors[b]
        folded = sum(product[:, g : g + LANES] for g in range(0, width, LANES))
        row = offset + index
        out_ref[row : row + 1, :] += jnp.sum(folded, axis=0, keepdims=True)


def gram(kept, got, offset, before, after=()):
    sources, _, own, wide = kept.shape
    args = [block.reshape(sources, own, wide) for block in (kept, got)]
    if before is not None:
        args.append(before)
    return call(
        functools.partial(gram_kernel, offset),
        "gram",
        [half((2 * sources, own, wide)), jax.ShapeDtypeStruct((2 * stat_rows(2 * sources), LANES), jnp.float32)],
        args,
        after,
    )


def pairs_of(count):
    return [(a, b) for a in range(count) for b in range(a, count)]


def stat_rows(count):
    return -(-len(pairs_of(count)) // 8) * 8


def adasum_coefs(table, count):
    def dot(first, second):
        total = 0.0
        for i, u in first.items():
            for j, v in second.items():
                total = total + u * v * table[min(i, j), max(i, j)]
        return total

    held = [{o: jnp.ones((1, LANES), jnp.float32)} for o in range(count)]
    while len(held) > 1:
        merged = []
        for low, high in zip(held[::2], held[1::2]):
            cross = dot(low, high)
            low_coef = 1.0 - cross / (2.0 * (jnp.maximum(dot(low, low), 0.0) + EPS))
            high_coef = 1.0 - cross / (2.0 * (jnp.maximum(dot(high, high), 0.0) + EPS))
            both = {o: low_coef * u for o, u in low.items()}
            both.update({o: high_coef * u for o, u in high.items()})
            merged.append(both)
        held = merged
    return held[0]


def finish_kernel(pieces, *refs):
    stats_ref = refs[0]
    conv_refs = refs[1 : 1 + pieces]
    expand_ref, conv_m_ref, expand_m_ref, conv_out, expand_out = refs[1 + pieces :]
    count, rows, _ = expand_ref.shape

    def apply(offset, v_refs, m_ref, out_ref):
        table = {}
        for index, pair in enumerate(pairs_of(count)):
            lane = stats_ref[offset + index : offset + index + 1, :]
            table[pair] = jnp.broadcast_to(jnp.sum(lane, axis=1, keepdims=True), (1, LANES))
        coefs = adasum_coefs(table, count)
        stride = sum(ref.shape[2] for ref in v_refs) // LANES
        group = 0
        for ref in v_refs:
            for start in range(0, ref.shape[2], LANES):
                total = sum(
                    coefs[o] * ref[o, :, start : start + LANES].astype(jnp.float32) for o in range(count)
                )
                place = pl.ds(group, rows, stride=stride)
                out_ref[place, :] = MOMENTUM * m_ref[place, :] + total
                group += 1

    apply(0, conv_refs, conv_m_ref, conv_out)
    apply(stat_rows(count), (expand_ref,), expand_m_ref, expand_out)


def finish(stats, conv_pieces, expand, conv_momentum, expand_momentum):
    conv_m = conv_momentum.reshape(-1, LANES)
    expand_m = expand_momentum.reshape(-1, LANES)
    conv_new, expand_new = pl.pallas_call(
        functools.partial(finish_kernel, len(conv_pieces)),
        out_shape=(
            jax.ShapeDtypeStruct(conv_m.shape, jnp.float32),
            jax.ShapeDtypeStruct(expand_m.shape, jnp.float32),
        ),
        compiler_params=params(),
        name="finish",
    )(stats, *conv_pieces, expand, conv_m, expand_m)
    return conv_new.reshape(conv_momentum.shape), expand_new.reshape(expand_momentum.shape)


def body(inputs, cotangent, conv_weight, expand_weight, conv_momentum, expand_momentum):
    shape = inputs.shape
    images, height, across, channels = shape
    rows = images * height * across
    wide = cotangent.shape[-1]
    outer_count = lax.axis_size("outer")
    inner_count = lax.axis_size("inner")
    inner_bits = inner_count.bit_length() - 1
    outer_bits = outer_count.bit_length() - 1
    own = conv_weight.shape[1] // (outer_count * inner_count)
    top = outer_bits - 1

    x_own = inputs.reshape(rows, channels)
    cut = images // 2 * height * across
    x_first = exchange(x_own[:cut], "inner", 0)
    x_second = exchange(x_own[cut:], "inner", 0)
    cot = cotangent.reshape(rows, wide)

    hidden, expand = [], []
    for index in range(2):
        block, send, keep = front(index, x_own, conv_weight, cot, shape, 1, own)
        hidden.append(block)
        expand.append((keep, exchange(send, "inner", 1)))
    hidden_grad, d_send, d_own = hidden_gradient(hidden, cot, expand_weight, own, (x_first,))
    d_other = exchange(d_send, "inner", 0)
    input_grad = backward(hidden_grad, conv_weight, x_own, shape).reshape(shape)

    parts = expand
    halves = outer_count // 2
    for bit in range(2, inner_bits):
        lead = halves << (inner_bits - 1 - bit)
        merged = []
        for kept, got in parts:
            shaped = [b.reshape(-1, 2, own, wide) for b in (kept, got)]
            send, keep = merge([shaped], [lead], "inner", bit, name="merge_expand_z")
            merged.append((keep, exchange(send, "inner", bit)))
        parts = merged
    early = [keep for keep, _ in parts]

    def to_owner(send, keep, after):
        got = exchange(send, "outer", top)
        for bit in reversed(range(top)):
            send, keep = spread(keep, got, bit, after)
            got = exchange(send, "outer", bit)
        return keep, got

    conv = []
    for tap_y in range(3):
        after = tuple(early) + (input_grad,) if tap_y == 0 else ()
        send, keep = kernel_grad(tap_y, (x_own, x_first, x_second), (d_own, d_other), shape, 1, own, after)
        conv.append((keep, exchange(send, "inner", 1)))

    shaped = [[b.reshape(-1, own, wide) for b in pair] for pair in parts]
    send, keep = merge(shaped, [halves] * 2, "inner", 0, name="merge_expand_y")
    expand_y = (keep, exchange(send, "inner", 0))

    stats = None
    ready = []
    expand_all = None
    for tap_y, (keep, got) in enumerate(conv):
        for bit in range(2, inner_bits):
            lead = outer_count << (inner_bits - 1 - bit)
            shaped = [b.reshape(-1, own, 3 * channels) for b in (keep, got)]
            after = (expand_y[0],) if tap_y == 0 else ()
            send, keep = merge([shaped], [lead], "inner", bit, after, name="merge_conv_z")
            got = exchange(send, "inner", bit)
        ready.append((keep, got))

    shaped = [b.reshape(-1, own, wide) for b in expand_y]
    send, keep = merge([shaped], [1], "outer", top, name="merge_expand_x")
    kept, got = to_owner(send, keep, ())
    expand_all, stats = gram(kept, got, stat_rows(outer_count), None)

    conv_all = []
    for tap_y, (keep, got) in enumerate(ready):
        shaped = [b.reshape(-1, own, 3 * channels) for b in (keep, got)]
        after = (stats,)
        send, keep = merge([shaped], [1], "outer", top, after, name="merge_conv_x")
        kept, got = to_owner(send, keep, ())
        vectors, stats = gram(kept, got, 0, stats)
        conv_all.append(vectors)

    for axis, bits in (("inner", inner_bits), ("outer", outer_bits)):
        for bit in range(bits):
            stats = stats + exchange(stats, axis, bit)
    conv_new, expand_new = finish(stats, conv_all, expand_all, conv_momentum, expand_momentum)
    return (input_grad, conv_new, expand_new)


def solution(mesh):
    split = P(("outer", "inner"))
    return jax.shard_map(
        body,
        mesh=mesh,
        in_specs=(split, split, P(), P(), split, split),
        out_specs=(split, split, split),
        check_vma=False,
    )
```

```python
import functools

import jax
import jax.numpy as jnp
from jax import lax
from jax.experimental import pallas as pl
from jax.experimental.pallas import tpu as pltpu
from jax.sharding import PartitionSpec as P

EPS = 1e-06
MOMENTUM = 0.9
LANES = 128
VMEM = 48 * 1024 * 1024


def params(**more):
    return pltpu.CompilerParams(vmem_limit_bytes=VMEM, **more)


def call(kernel, name, out_shape, args, after=(), scratch=(), in_specs=None):
    count = len(args)

    def run(*refs):
        kernel(*refs[:count], *refs[count + len(after) :])

    if in_specs is None:
        in_specs = [pl.BlockSpec(memory_space=pltpu.VMEM)] * count
    return pl.pallas_call(
        run,
        out_shape=out_shape,
        in_specs=list(in_specs) + [pl.BlockSpec(memory_space=pl.ANY)] * len(after),
        scratch_shapes=list(scratch),
        compiler_params=params(),
        cost_estimate=pl.CostEstimate(flops=1, bytes_accessed=1, transcendentals=0),
        name=name,
    )(*args, *after)


def half(shape):
    return jax.ShapeDtypeStruct(shape, jnp.bfloat16)


def exchange(block, axis, bit):
    count = lax.axis_size(axis)
    return lax.ppermute(block, axis, [(i, i ^ (1 << bit)) for i in range(count)])


def my_bit(axis, bit):
    return (lax.axis_index(axis) >> bit) & 1


def fill_row_taps(source_ref, taps_ref, images, height, across, relu):
    channels = source_ref.shape[1]
    area = height * across
    for image in range(images):
        base = image * area
        block = source_ref[base : base + area, :]
        if relu:
            block = jnp.maximum(block, jnp.zeros((), block.dtype))
        blank = jnp.zeros((across, channels), block.dtype)
        taps_ref[base : base + across, 0:channels] = blank
        taps_ref[base + across : base + area, 0:channels] = block[: area - across]
        taps_ref[base : base + area, channels : 2 * channels] = block
        taps_ref[base : base + area - across, 2 * channels : 3 * channels] = block[across:]
        taps_ref[base + area - across : base + area, 2 * channels : 3 * channels] = blank


def shifted_sum(product, across):
    rows, width = product(1).shape
    place = lax.rem(lax.broadcasted_iota(jnp.int32, (rows, width), 0), across)
    total = product(1)
    total += jnp.where(place > 0, pltpu.roll(product(0), 1, 0), 0.0)
    total += jnp.where(place < across - 1, pltpu.roll(product(2), rows - 1, 0), 0.0)
    return total


def store_split(value, bit, step, send_ref, keep_ref, first, columns):
    mine = my_bit("inner", bit)
    for pair in range(value.shape[0] // (2 * step)):
        zero = value[2 * pair * step : (2 * pair + 1) * step]
        one = value[(2 * pair + 1) * step : (2 * pair + 2) * step]
        place = slice(first + pair * step, first + (pair + 1) * step)
        keep_ref[place, columns] = jnp.where(mine == 0, zero, one).astype(keep_ref.dtype)
        send_ref[place, columns] = jnp.where(mine == 0, one, zero).astype(send_ref.dtype)


def split_rows(block, bit, step):
    mine = my_bit("inner", bit)
    parts = block.reshape(block.shape[0] // (2 * step), 2, step, block.shape[1])
    send = lax.dynamic_index_in_dim(parts, 1 - mine, 1, keepdims=False)
    keep = lax.dynamic_index_in_dim(parts, mine, 1, keepdims=False)
    return [part.reshape(block.shape[0] // 2, block.shape[1]) for part in (send, keep)]


def fused_split(own):
    return own % 16 == 0


def front_kernel(index, bit, own, shape, x_hbm, w_hbm, cot_hbm, *refs):
    images, height, across, channels = shape
    hid_ref, *out_refs = refs[:-5]
    x_ref, w_ref, cot_ref, taps_ref, sems = refs[-5:]
    rows, block = hid_ref.shape
    x_copy = pltpu.make_async_copy(x_hbm, x_ref, sems.at[0])
    cot_copy = pltpu.make_async_copy(cot_hbm, cot_ref, sems.at[1])
    w_copies = {}
    for tap_x in (1, 0, 2):
        for tap_y in range(3):
            tap = 3 * tap_y + tap_x
            w_copies[tap] = pltpu.make_async_copy(
                w_hbm.at[pl.ds(tap * channels, channels), pl.ds(index * block, block)],
                w_ref.at[pl.ds(tap * channels, channels), :],
                sems.at[2 + tap],
            )
    x_copy.start()
    for copy in w_copies.values():
        copy.start()
    cot_copy.start()
    x_copy.wait()
    fill_row_taps(x_ref, taps_ref, images, height, across, True)

    @functools.cache
    def product(tap_x):
        for tap_y in range(3):
            w_copies[3 * tap_y + tap_x].wait()
        weight = jnp.concatenate(
            [w_ref[(3 * tap_y + tap_x) * channels : (3 * tap_y + tap_x + 1) * channels, :] for tap_y in range(3)],
            axis=0,
        )
        return jnp.dot(taps_ref[...], weight, preferred_element_type=jnp.float32)

    hidden = shifted_sum(product, across).astype(hid_ref.dtype)
    hid_ref[...] = hidden
    act = jnp.maximum(hidden, jnp.zeros((), hidden.dtype))
    cot_copy.wait()
    wide = cot_ref.shape[1]
    piece = min(wide, 512)
    for start in range(0, wide, piece):
        columns = slice(start, start + piece)
        grad = lax.dot_general(
            act, cot_ref[:, columns], (((0,), (0,)), ((), ())), preferred_element_type=jnp.float32
        )
        grad = grad / rows
        if len(out_refs) == 2:
            store_split(grad, bit, own << bit, *out_refs, 0, columns)
        else:
            out_refs[0][:, columns] = grad.astype(jnp.bfloat16)


def front(index, x, weight, cot, shape, bit, own):
    rows, channels = x.shape
    wide = cot.shape[1]
    block = weight.shape[1] // 2
    parts = 2 if fused_split(own) else 1
    hidden, *grads = call(
        functools.partial(front_kernel, index, bit, own, shape),
        f"forward_expand{index}",
        [half((rows, block))] + [half((block // parts, wide))] * parts,
        (x, weight, cot),
        in_specs=[pl.BlockSpec(memory_space=pl.ANY)] * 3,
        scratch=[
            pltpu.VMEM((rows, channels), jnp.bfloat16),
            pltpu.VMEM((9 * channels, block), jnp.bfloat16),
            pltpu.VMEM((rows, wide), jnp.bfloat16),
            pltpu.VMEM((rows, 3 * channels), jnp.bfloat16),
            pltpu.SemaphoreType.DMA((11,)),
        ],
    )
    if parts == 1:
        grads = split_rows(grads[0], bit, own << bit)
    return hidden, *grads


def hidden_grad_kernel(own, *refs):
    blocks = refs[:2]
    cot_ref, w_ref, out_ref, *t_refs = refs[2:]
    wide = blocks[0].shape[1]
    for index, hid_ref in enumerate(blocks):
        place = slice(index * wide, (index + 1) * wide)
        back = lax.dot_general(
            cot_ref[...], w_ref[place, :], (((1,), (1,)), ((), ())), preferred_element_type=jnp.float32
        )
        grad = jnp.where(hid_ref[...].astype(jnp.float32) > 0, back, 0.0)
        out_ref[:, place] = grad.astype(out_ref.dtype)
        turned = grad.T
        if len(t_refs) == 2:
            store_split(turned, 0, own, *t_refs, index * wide // 2, slice(None))
        else:
            t_refs[0][place, :] = turned.astype(jnp.bfloat16)


def hidden_gradient(hidden, cot, weight, own, after):
    rows, block = hidden[0].shape
    wide = 2 * block
    parts = 2 if fused_split(own) else 1
    grad, *turned = call(
        functools.partial(hidden_grad_kernel, own),
        "hidden_grad",
        [half((rows, wide))] + [half((wide // parts, rows))] * parts,
        (*hidden, cot, weight),
        after,
    )
    if parts == 1:
        turned = split_rows(turned[0], 0, own)
    return grad, *turned


def backward_kernel(shape, d_ref, w_ref, x_ref, out_ref, token_ref, taps_ref):
    token_ref[...] = jnp.zeros(token_ref.shape, token_ref.dtype)
    images, height, across, channels = shape
    fill_row_taps(d_ref, taps_ref, images, height, across, False)
    block = channels // 2
    for start in range(0, channels, block):
        columns = slice(start, start + block)

        @functools.cache
        def product(tap_x):
            weight = jnp.concatenate(
                [w_ref[3 * (2 - tap_y) + 2 - tap_x, columns, :] for tap_y in range(3)], axis=1
            )
            return lax.dot_general(
                taps_ref[...], weight, (((1,), (1,)), ((), ())), preferred_element_type=jnp.float32
            )

        total = shifted_sum(product, across)
        keep = x_ref[:, columns].astype(jnp.float32) > 0
        out_ref[:, columns] = jnp.where(keep, total, 0.0).astype(out_ref.dtype)


def backward(hidden_grad, weight, x, shape, after):
    rows, channels = x.shape
    wide = weight.shape[1]
    return call(
        functools.partial(backward_kernel, shape),
        "conv_backward",
        [half((rows, channels)), jax.ShapeDtypeStruct((8, LANES), jnp.float32)],
        (hidden_grad, weight.reshape(9, channels, wide), x),
        after,
        scratch=[pltpu.VMEM((rows, 3 * wide), jnp.bfloat16)],
    )


def kernel_grad_kernel(taps, bit, step, shape, x_count, *refs):
    images, height, across, channels = shape
    area = height * across
    x_refs = refs[:x_count]
    d_refs = refs[x_count : x_count + 2]
    out_refs = refs[x_count + 2 : -2]
    x_ref, d_ref = refs[-2:]
    rows = d_refs[0].shape[1]

    def fill(tap_y):
        first = 0
        for ref in x_refs:
            for image in range(ref.shape[0] // area):
                block = ref[image * area : (image + 1) * area, :]
                block = jnp.maximum(block, jnp.zeros((), block.dtype))
                blank = jnp.zeros((across, channels), block.dtype)
                if tap_y == 0:
                    x_ref[first : first + across, :] = blank
                    x_ref[first + across : first + area, :] = block[: area - across]
                elif tap_y == 1:
                    x_ref[first : first + area, :] = block
                else:
                    x_ref[first : first + area - across, :] = block[across:]
                    x_ref[first + area - across : first + area, :] = blank
                first += area

    place = lax.rem(lax.broadcasted_iota(jnp.int32, d_refs[0].shape, 1), across)
    filled = None
    for index, tap in enumerate(taps):
        tap_y, tap_x = divmod(tap, 3)
        if tap_y != filled:
            fill(tap_y)
            filled = tap_y
        for source, ref in enumerate(d_refs):
            block = ref[...]
            if tap_x != 1:
                wide = pltpu.roll(block.astype(jnp.float32), (tap_x - 1) % rows, 1)
                valid = place < across - 1 if tap_x == 0 else place > 0
                block = jnp.where(valid, wide, 0.0).astype(block.dtype)
            d_ref[:, source * rows : (source + 1) * rows] = block
        total = jnp.dot(d_ref[...], x_ref[...], preferred_element_type=jnp.float32) / rows
        columns = slice(index * channels, (index + 1) * channels)
        if len(out_refs) == 2:
            store_split(total, bit, step, *out_refs, 0, columns)
        else:
            out_refs[0][:, columns] = total.astype(jnp.bfloat16)


def kernel_grad(taps, xs, ds, shape, bit, own, after):
    channels = shape[3]
    wide, rows = ds[0].shape
    parts = 2 if fused_split(own) else 1
    grads = call(
        functools.partial(kernel_grad_kernel, taps, bit, own << (bit - 1), shape, len(xs)),
        f"conv_grad_{taps[0]}_{taps[-1]}",
        [half((wide // parts, len(taps) * channels))] * parts,
        (*xs, *ds),
        after,
        scratch=[
            pltpu.VMEM((2 * rows, channels), jnp.bfloat16),
            pltpu.VMEM((wide, 2 * rows), jnp.bfloat16),
        ],
    )
    if parts == 1:
        grads = split_rows(grads[0], bit, own << (bit - 1))
    return grads


def added(kept, got):
    return kept.astype(jnp.float32) + got.astype(jnp.float32)


def merge_kernel(axis, bit, *refs):
    send_ref, keep_ref = refs[-2:]
    mine = my_bit(axis, bit)
    first = 0
    for kept, got in zip(refs[:-2:2], refs[1:-2:2]):
        columns = slice(first, first + kept.shape[-1])
        for out_ref, side in ((keep_ref, mine), (send_ref, 1 - mine)):
            out_ref[..., columns] = added(kept[:, side], got[:, side]).astype(out_ref.dtype)
        first = columns.stop


def merge_halves_kernel(axis, bit, *refs):
    send_ref, keep_ref = refs[-2:]
    mine = my_bit(axis, bit)
    zero, one = (added(kept[...], got[...]) for kept, got in zip(refs[:-2:2], refs[1:-2:2]))
    keep_ref[...] = jnp.where(mine == 0, zero, one).astype(keep_ref.dtype)
    send_ref[...] = jnp.where(mine == 0, one, zero).astype(send_ref.dtype)


def merge(parts, lead, axis, bit, name, after=(), halves=False):
    own = parts[0][0].shape[-2]
    sides = 1 if halves else 2
    flat = []
    for pair in parts:
        for block in pair:
            wide = block.shape[-1]
            shape = (lead, -1, own, wide) if halves else (lead, 2, block.size // (lead * 2 * own * wide), own, wide)
            flat.append(block.reshape(shape))
    middle = flat[0].shape[-3]
    wide = flat[0].shape[-1] if halves else sum(block.shape[-1] for block in flat[::2])
    kernel = merge_halves_kernel if halves else merge_kernel
    out = half((lead, middle, own, wide))
    send, keep = call(functools.partial(kernel, axis, bit), name, [out] * 2, flat, after)
    return keep, exchange(send, axis, bit)


def spread_kernel(bit, *refs):
    send_ref, keep_ref = refs[-2:]
    mine = my_bit("outer", bit)
    first = 0
    for kept, got in zip(refs[:-2:2], refs[1:-2:2]):
        columns = slice(first, first + kept.shape[-1])
        sources = kept.shape[0]
        for index, ref in enumerate((kept, got)):
            place = slice(index * sources, (index + 1) * sources)
            keep_ref[place, :, :, columns] = ref[:, mine]
            send_ref[place, :, :, columns] = ref[:, 1 - mine]
        first = columns.stop


def spread(parts, bit, name, after=()):
    sources, left, own, _ = parts[0][0].shape
    args = [block.reshape(sources, 2, left // 2, own, -1) for pair in parts for block in pair]
    out = half((2 * sources, left // 2, own, sum(block.shape[-1] for block in args[::2])))
    send, keep = call(functools.partial(spread_kernel, bit), name, [out] * 2, args, after)
    return keep, exchange(send, "outer", bit)


def gram_kernel(offset, has_before, last, *refs):
    kept, got = refs[:2]
    v_ref, out_ref = refs[2 + has_before : 4 + has_before]
    sources, rows, width = kept.shape
    count = 2 * sources
    levels = count.bit_length() - 1
    vectors = [None] * count
    for index in range(count):
        flips = sum(((index >> k) & 1) << (levels - 1 - k) for k in range(levels))
        vectors[flips] = (kept if index < sources else got)[index % sources].astype(jnp.float32)
    for bit in range(levels):
        mine = my_bit("outer", bit)
        for low in range(count):
            high = low | 1 << bit
            if high != low:
                a, b = vectors[low], vectors[high]
                vectors[low] = jnp.where(mine == 0, a, b)
                vectors[high] = jnp.where(mine == 0, b, a)
    for index, vector in enumerate(vectors):
        v_ref[index] = vector.astype(v_ref.dtype)
    if has_before:
        out_ref[...] = refs[2][...]
    else:
        out_ref[...] = jnp.zeros(out_ref.shape, jnp.float32)
    for index, (a, b) in enumerate(pairs_of(count)):
        product = vectors[a] * vectors[b]
        folded = sum(product[:, g : g + LANES] for g in range(0, width, LANES))
        row = offset + index
        out_ref[row : row + 1, :] += jnp.sum(folded, axis=0, keepdims=True)
    if last:
        row_ref = refs[4 + has_before]
        totals = jnp.sum(out_ref[...], axis=1, keepdims=True)
        rows = out_ref.shape[0]
        spot = lax.broadcasted_iota(jnp.int32, (rows, LANES), 1) == lax.broadcasted_iota(jnp.int32, (rows, LANES), 0)
        line = jnp.sum(jnp.where(spot, totals, 0.0), axis=0, keepdims=True)
        row_ref[...] = jnp.broadcast_to(line[None], row_ref.shape)


def gram(part, offset, before=None, devices=0):
    sources, _, own, wide = part[0].shape
    args = [block.reshape(sources, own, wide) for block in part]
    if before is not None:
        args.append(before)
    out = [half((2 * sources, own, wide)), jax.ShapeDtypeStruct((2 * stat_rows(2 * sources), LANES), jnp.float32)]
    if devices:
        out.append(jax.ShapeDtypeStruct((devices, 1, LANES), jnp.float32))
    return call(functools.partial(gram_kernel, offset, int(before is not None), devices > 0), "gram", out, args)


def pairs_of(count):
    return [(a, b) for a in range(count) for b in range(a, count)]


def stat_rows(count):
    return -(-len(pairs_of(count)) // 8) * 8


def adasum_coefs(table, count):
    def dot(first, second):
        total = 0.0
        for i, u in first.items():
            for j, v in second.items():
                total = total + u * v * table[min(i, j), max(i, j)]
        return total

    held = [{o: jnp.ones((1, LANES), jnp.float32)} for o in range(count)]
    while len(held) > 1:
        merged = []
        for low, high in zip(held[::2], held[1::2]):
            cross = dot(low, high)
            low_coef = 1.0 - cross / (2.0 * (jnp.maximum(dot(low, low), 0.0) + EPS))
            high_coef = 1.0 - cross / (2.0 * (jnp.maximum(dot(high, high), 0.0) + EPS))
            both = {o: low_coef * u for o, u in low.items()}
            both.update({o: high_coef * u for o, u in high.items()})
            merged.append(both)
        held = merged
    return held[0]


def finish_kernel(pieces, *refs):
    stats_ref = refs[0]
    conv_refs = refs[1 : 1 + pieces]
    expand_ref, conv_m_ref, expand_m_ref, conv_out, expand_out = refs[1 + pieces :]
    count, rows, _ = expand_ref.shape
    line = jnp.sum(stats_ref[...], axis=0)
    place_in_row = lax.broadcasted_iota(jnp.int32, line.shape, 1)

    def apply(offset, v_refs, m_ref, out_ref):
        table = {}
        for index, pair in enumerate(pairs_of(count)):
            value = jnp.sum(jnp.where(place_in_row == offset + index, line, 0.0), axis=1, keepdims=True)
            table[pair] = jnp.broadcast_to(value, (1, LANES))
        coefs = adasum_coefs(table, count)
        stride = sum(ref.shape[2] for ref in v_refs) // LANES
        group = 0
        for ref in v_refs:
            for start in range(0, ref.shape[2], LANES):
                total = sum(
                    coefs[o] * ref[o, :, start : start + LANES].astype(jnp.float32) for o in range(count)
                )
                place = pl.ds(group, rows, stride=stride)
                out_ref[place, :] = MOMENTUM * m_ref[place, :] + total
                group += 1

    apply(0, conv_refs, conv_m_ref, conv_out)
    apply(stat_rows(count), (expand_ref,), expand_m_ref, expand_out)


def finish(stats, conv_pieces, expand, conv_momentum, expand_momentum):
    conv_m = conv_momentum.reshape(-1, LANES)
    expand_m = expand_momentum.reshape(-1, LANES)
    conv_new, expand_new = pl.pallas_call(
        functools.partial(finish_kernel, len(conv_pieces)),
        out_shape=(
            jax.ShapeDtypeStruct(conv_m.shape, jnp.float32),
            jax.ShapeDtypeStruct(expand_m.shape, jnp.float32),
        ),
        compiler_params=params(),
        name="finish",
    )(stats, *conv_pieces, expand, conv_m, expand_m)
    return conv_new.reshape(conv_momentum.shape), expand_new.reshape(expand_momentum.shape)


def body(inputs, cotangent, conv_weight, expand_weight, conv_momentum, expand_momentum):
    shape = inputs.shape
    images, height, across, channels = shape
    rows = images * height * across
    wide = cotangent.shape[-1]
    outer_count = lax.axis_size("outer")
    inner_count = lax.axis_size("inner")
    inner_bits = inner_count.bit_length() - 1
    outer_bits = outer_count.bit_length() - 1
    own = conv_weight.shape[1] // (outer_count * inner_count)
    top = outer_bits - 1

    x_own = inputs.reshape(rows, channels)
    x_other = exchange(x_own, "inner", 0)
    cot = cotangent.reshape(rows, wide)

    hidden, expand = [], []
    for index in range(2):
        block, send, keep = front(index, x_own, conv_weight, cot, shape, 1, own)
        hidden.append(block)
        expand.append((keep, exchange(send, "inner", 1)))
    hidden_grad, d_send, d_own = hidden_gradient(hidden, cot, expand_weight, own, ())
    d_other = exchange(d_send, "inner", 0)

    lead = outer_count // 2
    first, second = (tuple(block.reshape(-1, own, wide) for block in part) for part in expand)
    after = (hidden_grad,)
    for bit in range(2, inner_bits):
        first = merge([first], lead << (inner_bits - 1 - bit), "inner", bit, "merge_first_z", after)
        after = (first[0],)
    input_grad, token = backward(hidden_grad, conv_weight, x_own, shape, (x_other, *after))
    second = merge([second], lead << (inner_bits - 2), "inner", 0, "merge_second_y", (token,))

    conv = []
    after = (second[0],)
    for taps in ((0, 1, 2, 3), (4, 5, 6), (7, 8)):
        send, keep = kernel_grad(taps, (x_own, x_other), (d_own, d_other), shape, 1, own, after)
        conv.append(tuple(b.reshape(-1, own, len(taps) * channels) for b in (keep, exchange(send, "inner", 1))))
        after = (keep,)
    first = merge([first], lead, "inner", 0, "merge_first_y", after)

    def along_z(part, lead, name, after):
        for bit in range(2, inner_bits):
            part = merge([part], lead << (inner_bits - 1 - bit), "inner", bit, name, after)
            after = (part[0],)
        return part

    def along_x(parts, name, after, halves=False):
        return merge(parts, 1, "outer", top, name, after, halves)

    def along_core(part, name, after):
        for bit in reversed(range(top)):
            part = spread([part], bit, name, after)
            after = (part[0],)
        return part

    at = stat_rows(outer_count)
    conv[0] = along_z(conv[0], outer_count, "merge_conv0_z", (first[0],))
    second = along_z(second, lead, "merge_second_z", (conv[0][0],))

    conv[1] = along_z(conv[1], outer_count, "merge_conv1_z", (second[0],))
    conv[0] = along_x(conv[:1], "merge_conv0_x", (conv[1][0],))
    expand = along_x([first, second], "merge_expand_x", (conv[0][0],), True)

    conv[2] = along_z(conv[2], outer_count, "merge_conv2_z", (expand[0],))
    conv[1] = along_x(conv[1:2], "merge_conv1_x", (conv[2][0],))
    expand = along_core(expand, "spread_expand", (conv[1][0],))
    conv[0] = along_core(conv[0], "spread_conv0", (expand[0],))

    conv[2] = along_x(conv[2:], "merge_conv2_x", (conv[0][0],))
    conv[1] = along_core(conv[1], "spread_conv1", (conv[2][0],))
    expand_all, stats = gram(expand, at)
    conv[0], stats = gram(conv[0], 0, stats)

    conv[2] = along_core(conv[2], "spread_conv2", (stats,))
    conv[1], stats = gram(conv[1], 0, stats)
    conv[2], _, row = gram(conv[2], 0, stats, outer_count * inner_count)
    stats = lax.all_to_all(row, ("outer", "inner"), 0, 0, tiled=True)
    conv_all = conv
    conv_new, expand_new = finish(stats, conv_all, expand_all, conv_momentum, expand_momentum)
    return (input_grad.reshape(shape), conv_new, expand_new)


def solution(mesh):
    split = P(("outer", "inner"))
    return jax.shard_map(
        body,
        mesh=mesh,
        in_specs=(split, split, P(), P(), split, split),
        out_specs=(split, split, split),
        check_vma=False,
    )
```

```python
import functools

import jax
import jax.numpy as jnp
from jax import lax
from jax.experimental import pallas as pl
from jax.experimental.pallas import tpu as pltpu
from jax.sharding import PartitionSpec as P

EPS = 1e-06
MOMENTUM = 0.9
LANES = 128
VMEM = 48 * 1024 * 1024


def params(**more):
    return pltpu.CompilerParams(vmem_limit_bytes=VMEM, **more)


def call(kernel, name, out_shape, args, after=(), scratch=(), in_specs=None):
    count = len(args)

    def run(*refs):
        kernel(*refs[:count], *refs[count + len(after) :])

    if in_specs is None:
        in_specs = [pl.BlockSpec(memory_space=pltpu.VMEM)] * count
    return pl.pallas_call(
        run,
        out_shape=out_shape,
        in_specs=list(in_specs) + [pl.BlockSpec(memory_space=pl.ANY)] * len(after),
        scratch_shapes=list(scratch),
        compiler_params=params(),
        cost_estimate=pl.CostEstimate(flops=1, bytes_accessed=1, transcendentals=0),
        name=name,
    )(*args, *after)


def half(shape):
    return jax.ShapeDtypeStruct(shape, jnp.bfloat16)


def exchange(block, axis, bit):
    count = lax.axis_size(axis)
    return lax.ppermute(block, axis, [(i, i ^ (1 << bit)) for i in range(count)])


def my_bit(axis, bit):
    return (lax.axis_index(axis) >> bit) & 1


def fill_row_taps(source_ref, taps_ref, images, height, across, relu):
    channels = source_ref.shape[1]
    area = height * across
    for image in range(images):
        base = image * area
        block = source_ref[base : base + area, :]
        if relu:
            block = jnp.maximum(block, jnp.zeros((), block.dtype))
        blank = jnp.zeros((across, channels), block.dtype)
        taps_ref[base : base + across, 0:channels] = blank
        taps_ref[base + across : base + area, 0:channels] = block[: area - across]
        taps_ref[base : base + area, channels : 2 * channels] = block
        taps_ref[base : base + area - across, 2 * channels : 3 * channels] = block[across:]
        taps_ref[base + area - across : base + area, 2 * channels : 3 * channels] = blank


def shifted_sum(product, across):
    rows, width = product(1).shape
    place = lax.rem(lax.broadcasted_iota(jnp.int32, (rows, width), 0), across)
    total = product(1)
    total += jnp.where(place > 0, pltpu.roll(product(0), 1, 0), 0.0)
    total += jnp.where(place < across - 1, pltpu.roll(product(2), rows - 1, 0), 0.0)
    return total


def store_split(value, bit, step, send_ref, keep_ref, first, columns):
    mine = my_bit("inner", bit)
    for pair in range(value.shape[0] // (2 * step)):
        zero = value[2 * pair * step : (2 * pair + 1) * step]
        one = value[(2 * pair + 1) * step : (2 * pair + 2) * step]
        place = slice(first + pair * step, first + (pair + 1) * step)
        keep_ref[place, columns] = jnp.where(mine == 0, zero, one).astype(keep_ref.dtype)
        send_ref[place, columns] = jnp.where(mine == 0, one, zero).astype(send_ref.dtype)


def split_rows(block, bit, step):
    mine = my_bit("inner", bit)
    parts = block.reshape(block.shape[0] // (2 * step), 2, step, block.shape[1])
    send = lax.dynamic_index_in_dim(parts, 1 - mine, 1, keepdims=False)
    keep = lax.dynamic_index_in_dim(parts, mine, 1, keepdims=False)
    return [part.reshape(block.shape[0] // 2, block.shape[1]) for part in (send, keep)]


def fused_split(own):
    return own % 16 == 0


def front_kernel(index, bit, own, shape, x_hbm, w_hbm, cot_hbm, *refs):
    images, height, across, channels = shape
    hid_ref, *out_refs = refs[:-5]
    x_ref, w_ref, cot_ref, taps_ref, sems = refs[-5:]
    rows, block = hid_ref.shape
    x_copy = pltpu.make_async_copy(x_hbm, x_ref, sems.at[0])
    cot_copy = pltpu.make_async_copy(cot_hbm, cot_ref, sems.at[1])
    w_copies = {}
    for tap_x in (1, 0, 2):
        for tap_y in range(3):
            tap = 3 * tap_y + tap_x
            w_copies[tap] = pltpu.make_async_copy(
                w_hbm.at[pl.ds(tap * channels, channels), pl.ds(index * block, block)],
                w_ref.at[pl.ds(tap * channels, channels), :],
                sems.at[2 + tap],
            )
    x_copy.start()
    for copy in w_copies.values():
        copy.start()
    cot_copy.start()
    x_copy.wait()
    fill_row_taps(x_ref, taps_ref, images, height, across, True)

    @functools.cache
    def product(tap_x):
        for tap_y in range(3):
            w_copies[3 * tap_y + tap_x].wait()
        weight = jnp.concatenate(
            [w_ref[(3 * tap_y + tap_x) * channels : (3 * tap_y + tap_x + 1) * channels, :] for tap_y in range(3)],
            axis=0,
        )
        return jnp.dot(taps_ref[...], weight, preferred_element_type=jnp.float32)

    hidden = shifted_sum(product, across).astype(hid_ref.dtype)
    hid_ref[...] = hidden
    act = jnp.maximum(hidden, jnp.zeros((), hidden.dtype))
    cot_copy.wait()
    wide = cot_ref.shape[1]
    piece = min(wide, 512)
    for start in range(0, wide, piece):
        columns = slice(start, start + piece)
        grad = lax.dot_general(
            act, cot_ref[:, columns], (((0,), (0,)), ((), ())), preferred_element_type=jnp.float32
        )
        grad = grad / rows
        if len(out_refs) == 2:
            store_split(grad, bit, own << bit, *out_refs, 0, columns)
        else:
            out_refs[0][:, columns] = grad.astype(jnp.bfloat16)


def front(index, x, weight, cot, shape, bit, own):
    rows, channels = x.shape
    wide = cot.shape[1]
    block = weight.shape[1] // 2
    parts = 2 if fused_split(own) else 1
    hidden, *grads = call(
        functools.partial(front_kernel, index, bit, own, shape),
        f"forward_expand{index}",
        [half((rows, block))] + [half((block // parts, wide))] * parts,
        (x, weight, cot),
        in_specs=[pl.BlockSpec(memory_space=pl.ANY)] * 3,
        scratch=[
            pltpu.VMEM((rows, channels), jnp.bfloat16),
            pltpu.VMEM((9 * channels, block), jnp.bfloat16),
            pltpu.VMEM((rows, wide), jnp.bfloat16),
            pltpu.VMEM((rows, 3 * channels), jnp.bfloat16),
            pltpu.SemaphoreType.DMA((11,)),
        ],
    )
    if parts == 1:
        grads = split_rows(grads[0], bit, own << bit)
    return hidden, *grads


def hidden_grad_kernel(own, *refs):
    blocks = refs[:2]
    cot_ref, w_ref, out_ref, *t_refs = refs[2:]
    wide = blocks[0].shape[1]
    for index, hid_ref in enumerate(blocks):
        place = slice(index * wide, (index + 1) * wide)
        back = lax.dot_general(
            cot_ref[...], w_ref[place, :], (((1,), (1,)), ((), ())), preferred_element_type=jnp.float32
        )
        grad = jnp.where(hid_ref[...].astype(jnp.float32) > 0, back, 0.0)
        out_ref[:, place] = grad.astype(out_ref.dtype)
        turned = grad.T
        if len(t_refs) == 2:
            store_split(turned, 0, own, *t_refs, index * wide // 2, slice(None))
        else:
            t_refs[0][place, :] = turned.astype(jnp.bfloat16)


def hidden_gradient(hidden, cot, weight, own, after):
    rows, block = hidden[0].shape
    wide = 2 * block
    parts = 2 if fused_split(own) else 1
    grad, *turned = call(
        functools.partial(hidden_grad_kernel, own),
        "hidden_grad",
        [half((rows, wide))] + [half((wide // parts, rows))] * parts,
        (*hidden, cot, weight),
        after,
    )
    if parts == 1:
        turned = split_rows(turned[0], 0, own)
    return grad, *turned


def backward_kernel(shape, d_ref, w_ref, x_ref, out_ref, token_ref, taps_ref):
    token_ref[...] = jnp.zeros(token_ref.shape, token_ref.dtype)
    images, height, across, channels = shape
    fill_row_taps(d_ref, taps_ref, images, height, across, False)
    block = channels // 2
    for start in range(0, channels, block):
        columns = slice(start, start + block)

        @functools.cache
        def product(tap_x):
            weight = jnp.concatenate(
                [w_ref[3 * (2 - tap_y) + 2 - tap_x, columns, :] for tap_y in range(3)], axis=1
            )
            return lax.dot_general(
                taps_ref[...], weight, (((1,), (1,)), ((), ())), preferred_element_type=jnp.float32
            )

        total = shifted_sum(product, across)
        keep = x_ref[:, columns].astype(jnp.float32) > 0
        out_ref[:, columns] = jnp.where(keep, total, 0.0).astype(out_ref.dtype)


def backward(hidden_grad, weight, x, shape, after):
    rows, channels = x.shape
    wide = weight.shape[1]
    return call(
        functools.partial(backward_kernel, shape),
        "conv_backward",
        [half((rows, channels)), jax.ShapeDtypeStruct((8, LANES), jnp.float32)],
        (hidden_grad, weight.reshape(9, channels, wide), x),
        after,
        scratch=[pltpu.VMEM((rows, 3 * wide), jnp.bfloat16)],
    )


def kernel_grad_kernel(taps, bit, step, shape, x_count, *refs):
    images, height, across, channels = shape
    area = height * across
    x_refs = refs[:x_count]
    d_refs = refs[x_count : x_count + 2]
    out_refs = refs[x_count + 2 : -2]
    x_ref, d_ref = refs[-2:]
    rows = d_refs[0].shape[1]

    def fill(tap_y):
        first = 0
        for ref in x_refs:
            for image in range(ref.shape[0] // area):
                block = ref[image * area : (image + 1) * area, :]
                block = jnp.maximum(block, jnp.zeros((), block.dtype))
                blank = jnp.zeros((across, channels), block.dtype)
                if tap_y == 0:
                    x_ref[first : first + across, :] = blank
                    x_ref[first + across : first + area, :] = block[: area - across]
                elif tap_y == 1:
                    x_ref[first : first + area, :] = block
                else:
                    x_ref[first : first + area - across, :] = block[across:]
                    x_ref[first + area - across : first + area, :] = blank
                first += area

    place = lax.rem(lax.broadcasted_iota(jnp.int32, d_refs[0].shape, 1), across)
    filled = None
    for index, tap in enumerate(taps):
        tap_y, tap_x = divmod(tap, 3)
        if tap_y != filled:
            fill(tap_y)
            filled = tap_y
        for source, ref in enumerate(d_refs):
            block = ref[...]
            if tap_x != 1:
                wide = pltpu.roll(block.astype(jnp.float32), (tap_x - 1) % rows, 1)
                valid = place < across - 1 if tap_x == 0 else place > 0
                block = jnp.where(valid, wide, 0.0).astype(block.dtype)
            d_ref[:, source * rows : (source + 1) * rows] = block
        total = jnp.dot(d_ref[...], x_ref[...], preferred_element_type=jnp.float32) / rows
        columns = slice(index * channels, (index + 1) * channels)
        if len(out_refs) == 2:
            store_split(total, bit, step, *out_refs, 0, columns)
        else:
            out_refs[0][:, columns] = total.astype(jnp.bfloat16)


def kernel_grad(taps, xs, ds, shape, bit, own, after):
    channels = shape[3]
    wide, rows = ds[0].shape
    parts = 2 if fused_split(own) else 1
    grads = call(
        functools.partial(kernel_grad_kernel, taps, bit, own << (bit - 1), shape, len(xs)),
        f"conv_grad_{taps[0]}_{taps[-1]}",
        [half((wide // parts, len(taps) * channels))] * parts,
        (*xs, *ds),
        after,
        scratch=[
            pltpu.VMEM((2 * rows, channels), jnp.bfloat16),
            pltpu.VMEM((wide, 2 * rows), jnp.bfloat16),
        ],
    )
    if parts == 1:
        grads = split_rows(grads[0], bit, own << (bit - 1))
    return grads


def added(kept, got):
    return kept.astype(jnp.float32) + got.astype(jnp.float32)


def merge_kernel(axis, bit, *refs):
    send_ref, keep_ref = refs[-2:]
    mine = my_bit(axis, bit)
    first = 0
    for kept, got in zip(refs[:-2:2], refs[1:-2:2]):
        columns = slice(first, first + kept.shape[-1])
        for out_ref, side in ((keep_ref, mine), (send_ref, 1 - mine)):
            out_ref[..., columns] = added(kept[:, side], got[:, side]).astype(out_ref.dtype)
        first = columns.stop


def merge_halves_kernel(axis, bit, kept, got, send_ref, keep_ref):
    mine = my_bit(axis, bit)
    wide = keep_ref.shape[-1]
    zero, one = (added(kept[..., columns], got[..., columns]) for columns in (slice(0, wide), slice(wide, 2 * wide)))
    keep_ref[...] = jnp.where(mine == 0, zero, one).astype(keep_ref.dtype)
    send_ref[...] = jnp.where(mine == 0, one, zero).astype(send_ref.dtype)


def merge(parts, lead, axis, bit, name, after=(), halves=False):
    own = parts[0][0].shape[-2]
    flat = []
    for pair in parts:
        for block in pair:
            wide = block.shape[-1]
            shape = (lead, -1, own, wide) if halves else (lead, 2, block.size // (lead * 2 * own * wide), own, wide)
            flat.append(block.reshape(shape))
    middle = flat[0].shape[-3]
    wide = sum(block.shape[-1] for block in flat[::2])
    if halves:
        wide //= 2
    kernel = merge_halves_kernel if halves else merge_kernel
    out = half((lead, middle, own, wide))
    send, keep = call(functools.partial(kernel, axis, bit), name, [out] * 2, flat, after)
    return keep, exchange(send, axis, bit)


def held_kernel(in_ref, out_ref):
    out_ref[...] = in_ref[...]


def held(block, after):
    return call(held_kernel, "held", half(block.shape), (block,), after)


def spread_kernel(bit, *refs):
    send_ref, keep_ref = refs[-2:]
    mine = my_bit("outer", bit)
    first = 0
    for kept, got in zip(refs[:-2:2], refs[1:-2:2]):
        columns = slice(first, first + kept.shape[-1])
        sources = kept.shape[0]
        for index, ref in enumerate((kept, got)):
            place = slice(index * sources, (index + 1) * sources)
            keep_ref[place, :, :, columns] = ref[:, mine]
            send_ref[place, :, :, columns] = ref[:, 1 - mine]
        first = columns.stop


def spread(parts, bit, name, after=()):
    sources, left, own, _ = parts[0][0].shape
    args = [block.reshape(sources, 2, left // 2, own, -1) for pair in parts for block in pair]
    out = half((2 * sources, left // 2, own, sum(block.shape[-1] for block in args[::2])))
    send, keep = call(functools.partial(spread_kernel, bit), name, [out] * 2, args, after)
    return keep, exchange(send, "outer", bit)


def gram_kernel(offset, has_before, last, *refs):
    kept, got = refs[:2]
    v_ref, out_ref = refs[2 + has_before : 4 + has_before]
    sources, rows, width = kept.shape
    count = 2 * sources
    levels = count.bit_length() - 1
    vectors = [None] * count
    for index in range(count):
        flips = sum(((index >> k) & 1) << (levels - 1 - k) for k in range(levels))
        vectors[flips] = (kept if index < sources else got)[index % sources].astype(jnp.float32)
    for bit in range(levels):
        mine = my_bit("outer", bit)
        for low in range(count):
            high = low | 1 << bit
            if high != low:
                a, b = vectors[low], vectors[high]
                vectors[low] = jnp.where(mine == 0, a, b)
                vectors[high] = jnp.where(mine == 0, b, a)
    for index, vector in enumerate(vectors):
        v_ref[index] = vector.astype(v_ref.dtype)
    if has_before:
        out_ref[...] = refs[2][...]
    else:
        out_ref[...] = jnp.zeros(out_ref.shape, jnp.float32)
    for index, (a, b) in enumerate(pairs_of(count)):
        product = vectors[a] * vectors[b]
        folded = sum(product[:, g : g + LANES] for g in range(0, width, LANES))
        row = offset + index
        out_ref[row : row + 1, :] += jnp.sum(folded, axis=0, keepdims=True)
    if last:
        row_ref = refs[4 + has_before]
        totals = jnp.sum(out_ref[...], axis=1, keepdims=True)
        rows = out_ref.shape[0]
        spot = lax.broadcasted_iota(jnp.int32, (rows, LANES), 1) == lax.broadcasted_iota(jnp.int32, (rows, LANES), 0)
        line = jnp.sum(jnp.where(spot, totals, 0.0), axis=0, keepdims=True)
        row_ref[...] = jnp.broadcast_to(line[None], row_ref.shape)


def gram(part, offset, before=None, devices=0):
    sources, _, own, wide = part[0].shape
    args = [block.reshape(sources, own, wide) for block in part]
    if before is not None:
        args.append(before)
    out = [half((2 * sources, own, wide)), jax.ShapeDtypeStruct((2 * stat_rows(2 * sources), LANES), jnp.float32)]
    if devices:
        out.append(jax.ShapeDtypeStruct((devices, 1, LANES), jnp.float32))
    return call(functools.partial(gram_kernel, offset, int(before is not None), devices > 0), "gram", out, args)


def pairs_of(count):
    return [(a, b) for a in range(count) for b in range(a, count)]


def stat_rows(count):
    return -(-len(pairs_of(count)) // 8) * 8


def adasum_coefs(table, count):
    def dot(first, second):
        total = 0.0
        for i, u in first.items():
            for j, v in second.items():
                total = total + u * v * table[min(i, j), max(i, j)]
        return total

    held = [{o: jnp.ones((1, LANES), jnp.float32)} for o in range(count)]
    while len(held) > 1:
        merged = []
        for low, high in zip(held[::2], held[1::2]):
            cross = dot(low, high)
            low_coef = 1.0 - cross / (2.0 * (jnp.maximum(dot(low, low), 0.0) + EPS))
            high_coef = 1.0 - cross / (2.0 * (jnp.maximum(dot(high, high), 0.0) + EPS))
            both = {o: low_coef * u for o, u in low.items()}
            both.update({o: high_coef * u for o, u in high.items()})
            merged.append(both)
        held = merged
    return held[0]


def finish_kernel(pieces, *refs):
    stats_ref = refs[0]
    conv_refs = refs[1 : 1 + pieces]
    expand_ref, conv_m_ref, expand_m_ref, conv_out, expand_out = refs[1 + pieces :]
    count, rows, _ = expand_ref.shape
    line = jnp.sum(stats_ref[...], axis=0)
    place_in_row = lax.broadcasted_iota(jnp.int32, line.shape, 1)

    def apply(offset, v_refs, m_ref, out_ref):
        table = {}
        for index, pair in enumerate(pairs_of(count)):
            value = jnp.sum(jnp.where(place_in_row == offset + index, line, 0.0), axis=1, keepdims=True)
            table[pair] = jnp.broadcast_to(value, (1, LANES))
        coefs = adasum_coefs(table, count)
        stride = sum(ref.shape[2] for ref in v_refs) // LANES
        group = 0
        for ref in v_refs:
            for start in range(0, ref.shape[2], LANES):
                total = sum(
                    coefs[o] * ref[o, :, start : start + LANES].astype(jnp.float32) for o in range(count)
                )
                place = pl.ds(group, rows, stride=stride)
                out_ref[place, :] = MOMENTUM * m_ref[place, :] + total
                group += 1

    apply(0, conv_refs, conv_m_ref, conv_out)
    apply(stat_rows(count), (expand_ref,), expand_m_ref, expand_out)


def finish(stats, conv_pieces, expand, conv_momentum, expand_momentum):
    conv_m = conv_momentum.reshape(-1, LANES)
    expand_m = expand_momentum.reshape(-1, LANES)
    conv_new, expand_new = pl.pallas_call(
        functools.partial(finish_kernel, len(conv_pieces)),
        out_shape=(
            jax.ShapeDtypeStruct(conv_m.shape, jnp.float32),
            jax.ShapeDtypeStruct(expand_m.shape, jnp.float32),
        ),
        compiler_params=params(),
        name="finish",
    )(stats, *conv_pieces, expand, conv_m, expand_m)
    return conv_new.reshape(conv_momentum.shape), expand_new.reshape(expand_momentum.shape)


def body(inputs, cotangent, conv_weight, expand_weight, conv_momentum, expand_momentum):
    shape = inputs.shape
    images, height, across, channels = shape
    rows = images * height * across
    wide = cotangent.shape[-1]
    outer_count = lax.axis_size("outer")
    inner_count = lax.axis_size("inner")
    inner_bits = inner_count.bit_length() - 1
    outer_bits = outer_count.bit_length() - 1
    own = conv_weight.shape[1] // (outer_count * inner_count)
    top = outer_bits - 1

    x_own = inputs.reshape(rows, channels)
    x_other = exchange(x_own, "inner", 0)
    cot = cotangent.reshape(rows, wide)

    hidden, expand = [], []
    for index in range(2):
        block, send, keep = front(index, x_own, conv_weight, cot, shape, 1, own)
        hidden.append(block)
        expand.append((keep, exchange(send, "inner", 1)))
    hidden_grad, d_send, d_own = hidden_gradient(hidden, cot, expand_weight, own, ())
    d_other = exchange(d_send, "inner", 0)

    lead = outer_count // 2
    expand = [tuple(block.reshape(-1, own, wide) for block in part) for part in expand]
    input_grad, token = backward(hidden_grad, conv_weight, x_own, shape, (x_other,))
    expand = merge(expand, lead << (inner_bits - 2), "inner", 0, "merge_expand_y", (token,))

    conv = []
    after = (expand[0],)
    for taps in ((0, 1, 2), (3, 4, 5, 6), (7, 8)):
        send, keep = kernel_grad(taps, (x_own, x_other), (d_own, d_other), shape, 1, own, after)
        conv.append((send.reshape(-1, own, len(taps) * channels), keep.reshape(-1, own, len(taps) * channels)))
        after = (keep,)

    def start(index, after):
        send, keep = conv[index]
        conv[index] = (keep, exchange(held(send, after) if after else send, "inner", 1))

    def along_z(part, lead, name, after):
        for bit in range(2, inner_bits):
            part = merge([part], lead << (inner_bits - 1 - bit), "inner", bit, name, after)
            after = (part[0],)
        return part

    def along_x(parts, name, after, halves=False):
        return merge(parts, 1, "outer", top, name, after, halves)

    def along_core(part, name, after):
        for bit in reversed(range(top)):
            part = spread([part], bit, name, after)
            after = (part[0],)
        return part

    at = stat_rows(outer_count)
    start(0, ())
    conv[0] = along_z(conv[0], outer_count, "merge_conv0_z", after)
    expand = along_z(expand, lead, "merge_expand_z", (conv[0][0],))

    start(1, (conv[0][0],))
    conv[1] = along_z(conv[1], outer_count, "merge_conv1_z", (expand[0],))
    conv[0] = along_x(conv[:1], "merge_conv0_x", (conv[1][0],))
    expand = along_x([expand], "merge_expand_x", (conv[0][0],), True)

    start(2, (conv[1][0],))
    conv[2] = along_z(conv[2], outer_count, "merge_conv2_z", (expand[0],))
    conv[1] = along_x(conv[1:2], "merge_conv1_x", (conv[2][0],))
    expand = along_core(expand, "spread_expand", (conv[1][0],))
    conv[0] = along_core(conv[0], "spread_conv0", (expand[0],))

    conv[2] = along_x(conv[2:], "merge_conv2_x", (conv[0][0],))
    conv[1] = along_core(conv[1], "spread_conv1", (conv[2][0],))
    expand_all, stats = gram(expand, at)
    conv[0], stats = gram(conv[0], 0, stats)

    conv[2] = along_core(conv[2], "spread_conv2", (stats,))
    conv[1], stats = gram(conv[1], 0, stats)
    conv[2], _, row = gram(conv[2], 0, stats, outer_count * inner_count)
    stats = lax.all_to_all(row, ("outer", "inner"), 0, 0, tiled=True)
    conv_all = conv
    conv_new, expand_new = finish(stats, conv_all, expand_all, conv_momentum, expand_momentum)
    return (input_grad.reshape(shape), conv_new, expand_new)


def solution(mesh):
    split = P(("outer", "inner"))
    return jax.shard_map(
        body,
        mesh=mesh,
        in_specs=(split, split, P(), P(), split, split),
        out_specs=(split, split, split),
        check_vma=False,
    )
```
